512 devices in a mesh: row: 32 (over z, y_lo), col: 16 (over y_hi, x, core).
Axes of the slice: x: 4, y: 4 (y_hi: 2, y_lo: 2; y = y_hi * 2 + y_lo), z: 16, core: 2. Of those that a mesh axis runs over, the one named last changes fastest.
Arguments:
- slab_t: bfloat16 [2, 1024, 98304], P(None, 'col', 'row'), may hold values from -6 to 6
- target_t: bfloat16 [2, 1024, 98304], P(None, 'col', 'row'), may hold values from -6 to 6
- factor_h: bfloat16 [2, 1024, 1024], P(None, 'row', 'col'), may hold values from -0.1875 to 0.1875
Outputs:
- gram_residual: float32 [1024, 2, 1024], P('row', None, 'col')
- polar_residual: float32 [2, 1024, 98304], P(None, 'col', 'row')
The draws below stay inside these ranges and needn't reach their ends.
All inputs are finite; a program needn't handle non-finite values.
Results may differ from the reference program's by a relative error of at most 0.0003.
Values may be sent and summed in bfloat16 or wider, within the bound.
No kernel may reach another device: no remote copies, remote signals or barrier semaphores. Data moves between devices by JAX's collectives and lax.ppermute only.
A program may use at most 64 MiB of HBM per device.

```python
import math
import jax
import jax.numpy as jnp
from jax import lax

W = 1024
SLABS = 2
N = 98304


def block_levels(own_key, dims, split, least, high):
    gain = 1.0
    for axis_at, parts in split:
        heights = jax.random.uniform(jax.random.fold_in(jax.random.fold_in(own_key, 6), axis_at), (parts,), jnp.float32, least / len(split), high / len(split))
        gain = gain * jnp.repeat(jnp.exp(heights), dims[axis_at] // parts).reshape((-1,) + (1,) * (len(dims) - 1 - axis_at))
    return gain


def gaussian(own_key, shape, deviation, reach, split=(), kind=jnp.bfloat16):
    array = jax.random.normal(own_key, shape, jnp.float32) * deviation
    if len(split) > 0:
        array = block_levels(own_key, shape, split, -0.22, 0.18) * array
    return jnp.clip(array, min=-reach, max=reach).astype(kind)


def setup_inputs(seed: int = 0) -> dict:
    seeds = jax.random.split(jax.random.key(seed), 4)
    slab_t = gaussian(seeds[0], (SLABS, W, N), 1.0, 6.0, ((1, 16), (2, 32)))
    target_t = gaussian(seeds[1], (SLABS, W, N), 1.0, 6.0, ((1, 16), (2, 32)))
    factor_h = gaussian(seeds[2], (SLABS, W, W), W ** -0.5, 0.1875, ((1, 32), (2, 16)))
    return dict(slab_t=slab_t, target_t=target_t, factor_h=factor_h)


def reference(slab_t, target_t, factor_h):
    scale = 1.0 / math.sqrt(N)

    def single(items):
        upper, target, factor = items
        upper32 = upper.astype(jnp.float32)
        gram = jnp.dot(upper32, upper32.T, precision=lax.Precision.HIGHEST)
        gram = (gram - N * jnp.eye(W, dtype=jnp.float32)) * scale
        recon = jnp.dot(factor.astype(jnp.float32).T, upper32, precision=lax.Precision.HIGHEST)
        return (gram, target.astype(jnp.float32) - recon)
    grams, polars = lax.map(single, (slab_t, target_t, factor_h))
    return (jnp.transpose(grams, (1, 0, 2)), polars)
```

```python
import math

import jax
import jax.numpy as jnp
from jax import lax
from jax.experimental import pallas as pl
from jax.experimental.pallas import tpu as pltpu
from jax.sharding import Mesh, PartitionSpec as P

AXES = ("z", "yl", "yh", "x", "c")
ROW = ("z", "yl")
COL = ("yh", "x", "c")
SWAP = [(0, 1), (1, 0)]


def shift(a, by):
    return lax.ppermute(a, "x", [(i, (i + by) % 4) for i in range(4)])


def products(index, own, a_mine, a_core, b_mine, b_core, h, recon, gram):
    width = 64
    mine = own[...]
    total = None
    for at, rows in enumerate((a_mine, a_core, b_mine, b_core)):
        block = rows[...]
        terms = lax.dot_general(block, mine, (((1,), (1,)), ((), ())), preferred_element_type=jnp.float32)
        picked = []
        for part in range(4):
            place = pl.ds(pl.multiple_of(index[at * 4 + part] * width, width), width)
            gram[place, :] = terms[part * width:(part + 1) * width]
            picked.append(h[place, :])
        factor = jnp.concatenate(picked, axis=0)
        term = lax.dot_general(factor, block, (((0,), (0,)), ((), ())), preferred_element_type=jnp.float32)
        if total is None:
            total = term
        else:
            total = total + term
    recon[...] = total


def shards(slab_t, target_t, factor_h):
    yh, x, c = (lax.axis_index(name) for name in COL)
    width, rows = slab_t.shape[1:]

    def pick(array, at):
        return lax.dynamic_index_in_dim(array, at, 0, keepdims=False)

    own = pick(slab_t, yh)
    other = lax.ppermute(pick(slab_t, 1 - yh), "yh", SWAP)
    h_other = lax.ppermute(pick(factor_h, 1 - yh), "yh", SWAP)
    h_mine = jnp.concatenate([pick(factor_h, yh), h_other], axis=1)

    def over_x(a):
        return jnp.concatenate([a, shift(a, 1), shift(a, -1), shift(a, 2)], axis=0)

    a_mine = over_x(own)
    b_mine = over_x(other)
    nrow = lax.axis_size(ROW)
    h_all = lax.all_to_all(jnp.broadcast_to(h_mine[None], (nrow,) + h_mine.shape), ROW, 0, 0, tiled=True)
    h_all = h_all.reshape(-1, 2 * width)
    a_core = lax.ppermute(a_mine, "c", SWAP)
    b_core = lax.ppermute(b_mine, "c", SWAP)

    at_x = jnp.stack([x, (x + 3) % 4, (x + 1) % 4, (x + 2) % 4])
    at_yc = jnp.stack([yh * 8 + c, yh * 8 + 1 - c, 8 - yh * 8 + c, 9 - yh * 8 - c])
    index = (at_yc[:, None] + 2 * at_x[None, :]).reshape(16).astype(jnp.int32)

    vmem = pl.BlockSpec(memory_space=pltpu.VMEM)
    recon, terms = pl.pallas_call(
        products,
        out_shape=(
            jax.ShapeDtypeStruct((2 * width, rows), jnp.float32),
            jax.ShapeDtypeStruct((16 * width, 2 * width), jnp.float32),
        ),
        in_specs=[pl.BlockSpec(memory_space=pltpu.SMEM)] + [vmem] * 6,
        out_specs=(vmem, vmem),
        compiler_params=pltpu.CompilerParams(vmem_limit_bytes=40 * 2**20),
        cost_estimate=pl.CostEstimate(flops=4 * 16 * 2 * width * width * rows, bytes_accessed=10 * 2**20, transcendentals=0),
    )(index, jnp.concatenate([own, other], axis=0), a_mine, a_core, b_mine, b_core, h_all)

    slab = jnp.arange(2, dtype=jnp.int32)
    recon_other = lax.ppermute(recon[width:], "yh", SWAP)
    is_own = (slab == yh)[:, None, None]
    polar = target_t.astype(jnp.float32) - jnp.where(is_own, recon[None, :width], recon_other[None])

    local = 16 * width // nrow
    summed = lax.all_to_all(terms.reshape(nrow, local, 2 * width), ROW, 0, 0, tiled=True).sum(0)
    gram_other = lax.ppermute(summed[:, width:], "yh", SWAP)
    gram = jnp.where((slab == yh)[None, :, None], summed[:, None, :width], gram_other[:, None])
    order_n = rows * nrow
    b_index = lax.axis_index(ROW) * local + jnp.arange(local, dtype=jnp.int32)
    a_index = lax.axis_index(COL) * width + jnp.arange(width, dtype=jnp.int32)
    identity = (b_index[:, None, None] == a_index[None, None, :]).astype(jnp.float32)
    gram = (gram - order_n * identity) * (1.0 / math.sqrt(order_n))
    return (gram, polar)


def solution(mesh):
    parts = Mesh(mesh.devices.reshape(16, 2, 2, 4, 2), AXES)
    return jax.shard_map(
        shards,
        mesh=parts,
        in_specs=(P(None, COL, ROW), P(None, COL, ROW), P(None, ROW, COL)),
        out_specs=(P(ROW, None, COL), P(None, COL, ROW)),
        check_vma=False,
    )
```

```python
import math

import jax
import jax.numpy as jnp
from jax import lax
from jax.experimental import pallas as pl
from jax.experimental.pallas import tpu as pltpu
from jax.sharding import Mesh, PartitionSpec as P

AXES = ("z", "yl", "yh", "x", "c")
ROW = ("z", "yl")
COL = ("yh", "x", "c")
SWAP = [(0, 1), (1, 0)]


def gram_products(index, mine, core, gram):
    width = gram.shape[2]
    runs = [pl.ds(pl.multiple_of((4 * yh + index[2]) * width, width), width) for yh in range(2)]
    own = jnp.concatenate([mine[run, :] for run in runs], axis=0)
    for rows, c in ((mine, index[1]), (core, 1 - index[1])):
        terms = lax.dot_general(rows[...], own, (((1,), (1,)), ((), ())), preferred_element_type=jnp.float32)
        gram[:, c] = terms.reshape(-1, width, 2 * width)


def recon_products(index, mine, core, h, h_yl, h_yh, h_both, keep, send):
    width = keep.shape[0]
    local = width // 2
    total = None
    for rows, c in ((mine, index[1]), (core, 1 - index[1])):
        picked = []
        for block in range(rows.shape[0] // width):
            at = pl.ds(pl.multiple_of((2 * block + c) * local, local), local)
            runs = []
            for ours, theirs in ((h, h_yh), (h_yl, h_both)):
                run = [jnp.where(index[0] == 0, part[at, :width], part[at, width:]) for part in (ours, theirs)]
                runs.append(jnp.concatenate(run, axis=1))
            picked.append(jnp.where(index[3] == 0, runs[0], runs[1]))
            picked.append(jnp.where(index[3] == 0, runs[1], runs[0]))
        factor = jnp.concatenate(picked, axis=0)
        term = lax.dot_general(factor, rows[...], (((0,), (0,)), ((), ())), preferred_element_type=jnp.float32)
        total = term if total is None else total + term
    send[...] = total[width:]
    keep[...] = total[:width]


def shards(slab_t, target_t, factor_h):
    yh, x, c = (lax.axis_index(name) for name in COL)
    yl = lax.axis_index("yl")
    width, rows = slab_t.shape[1:]
    nrow, nz, nx = lax.axis_size(ROW), lax.axis_size("z"), lax.axis_size("x")
    copies = jnp.broadcast_to(slab_t[:, None], (2, nx, width, rows)).reshape(2 * nx * width, rows)
    mine = lax.all_to_all(copies, ("yh", "x"), 0, 0, tiled=True)
    h_all = lax.all_gather(jnp.concatenate([factor_h[0], factor_h[1]], axis=1), "z", axis=0, tiled=True)
    h_yl = lax.ppermute(h_all, "yl", SWAP)
    h_yh = lax.ppermute(h_all, "yh", SWAP)
    h_both = lax.ppermute(h_all, ("yl", "yh"), [(i, 3 - i) for i in range(4)])
    mine, h_yl, h_yh, h_both = lax.optimization_barrier((mine, h_yl, h_yh, h_both))
    core = lax.ppermute(mine, "c", SWAP)

    index = jnp.stack([yh, c, x, yl]).astype(jnp.int32)
    smem, vmem = (pl.BlockSpec(memory_space=space) for space in (pltpu.SMEM, pltpu.VMEM))
    params = pltpu.CompilerParams(vmem_limit_bytes=40 * 2**20)
    cost = pl.CostEstimate(flops=2 * 16 * 2 * width * width * rows, bytes_accessed=8 * 2**20, transcendentals=0)
    half_like = jax.ShapeDtypeStruct((width, rows), jnp.float32)
    terms = pl.pallas_call(
        gram_products,
        out_shape=jax.ShapeDtypeStruct((2 * nx, 2, width, 2 * width), jnp.float32),
        in_specs=[smem] + [vmem] * 2,
        out_specs=vmem,
        compiler_params=params,
        cost_estimate=cost,
    )(index, mine, core)
    keep, send = pl.pallas_call(
        recon_products,
        out_shape=(half_like, half_like),
        in_specs=[smem] + [vmem] * 6,
        out_specs=(vmem,) * 2,
        compiler_params=params,
        cost_estimate=cost,
    )(index, mine, core, h_all, h_yl, h_yh, h_both)

    local = width // 2
    summed = lax.all_to_all(terms.reshape(nz, width, 2 * width), "z", 0, 0, tiled=True).sum(0)
    parts = summed.reshape(2, local, 2, width).transpose(0, 2, 1, 3).reshape(4, local, width)
    summed = lax.all_to_all(parts, ("yl", "yh"), 0, 0, tiled=True).reshape(2, 2, local, width).sum(0)

    slab = jnp.arange(2, dtype=jnp.int32)
    recon_other = lax.ppermute(send, "yh", SWAP)
    is_own = (slab == yh)[:, None, None]
    polar = target_t.astype(jnp.float32) - jnp.where(is_own, keep[None], recon_other[None])

    order_n = rows * nrow
    b_index = lax.axis_index(ROW) * local + jnp.arange(local, dtype=jnp.int32)
    a_index = lax.axis_index(COL) * width + jnp.arange(width, dtype=jnp.int32)
    identity = (b_index[:, None, None] == a_index[None, None, :]).astype(jnp.float32)
    gram = (summed.transpose(1, 0, 2) - order_n * identity) * (1.0 / math.sqrt(order_n))
    return (gram, polar)


def solution(mesh):
    parts = Mesh(mesh.devices.reshape(16, 2, 2, 4, 2), AXES)
    return jax.shard_map(
        shards,
        mesh=parts,
        in_specs=(P(None, COL, ROW), P(None, COL, ROW), P(None, ROW, COL)),
        out_specs=(P(ROW, None, COL), P(None, COL, ROW)),
        check_vma=False,
    )
```

```python
import functools
import itertools
import math

import jax
import jax.numpy as jnp
from jax import lax
from jax.experimental import pallas as pl
from jax.experimental.pallas import tpu as pltpu
from jax.sharding import Mesh, PartitionSpec as P

AXES = ("z", "yl", "yh", "x", "c")
ROW = ("z", "yl")
COL = ("yh", "x", "c")
SWAP = [(0, 1), (1, 0)]


def spread(slab, copies, sems):
    half = copies.shape[4]
    started = []
    for yh, x, c in itertools.product(*map(range, copies.shape[:3])):
        source = slab.at[yh, :, pl.ds(c * half, half)]
        started.append(pltpu.make_async_copy(source, copies.at[yh, x, c], sems.at[len(started)]))
        started[-1].start()
    for copy in started:
        copy.wait()


def gram_products(index, mine, core):
    width = mine.shape[0] // 16
    c = index[1] if core == 0 else 1 - index[1]
    own = [mine[pl.ds(pl.multiple_of((8 * yh + 2 * index[2] + c) * width, width), width), :] for yh in range(2)]
    own = jnp.concatenate(own, axis=0)
    terms = lax.dot_general(mine[...], own, (((1,), (1,)), ((), ())), preferred_element_type=jnp.float32)
    terms = terms.reshape(-1, 2, 2, width // 4, 2 * width)
    parts = []
    for yh in range(2):
        columns = terms[..., yh * width:(yh + 1) * width]
        parts.append(jnp.concatenate([columns[:, :, 0], columns[:, :, 1]], axis=-1))
    return parts


def other_core_gram(index, mine, gram):
    for yh, part in enumerate(gram_products(index, mine, 1)):
        gram[:, :, yh] = part


def this_core_gram(index, mine, received, keep, send):
    for yh, part in enumerate(gram_products(index, mine, 0)):
        total = part + received[:, :, yh]
        keep[:, yh] = jnp.where(index[3] == 0, total[:, 0], total[:, 1])
        send[:, yh] = jnp.where(index[3] == 0, total[:, 1], total[:, 0])


def arrange(index, h, h_yl, h_yh, h_both, factor):
    width = factor.shape[1] // 2
    halves = []
    for parts in ((h, h_yh), (h_yl, h_both)):
        runs = [jnp.where(index[0] == 0, part[:, :width], part[:, width:]) for part in parts]
        halves.append(jnp.concatenate(runs, axis=1))
    pair = [jnp.where(index[3] == yl, halves[0], halves[1]).reshape(-1, width // 2, 2 * width) for yl in range(2)]
    factor[...] = jnp.stack(pair, axis=1).reshape(factor.shape)


def recon_products(index, mine, core, factor, keep, send):
    width, half = keep.shape[0], mine.shape[1]
    for rows, c in ((mine, index[1]), (core, 1 - index[1])):
        total = lax.dot_general(factor[...], rows[...], (((0,), (0,)), ((), ())), preferred_element_type=jnp.float32)
        at = pl.ds(pl.multiple_of(c * half, half), half)
        send[:, at] = total[width:]
        keep[:, at] = total[:width]


def shards(slab_t, target_t, factor_h):
    yh, x, c = (lax.axis_index(name) for name in COL)
    yl = lax.axis_index("yl")
    width, rows = slab_t.shape[1:]
    nrow, nz, nx = lax.axis_size(ROW), lax.axis_size("z"), lax.axis_size("x")
    half = rows // 2
    smem, vmem, anywhere = (pl.BlockSpec(memory_space=space) for space in (pltpu.SMEM, pltpu.VMEM, pl.ANY))
    copies = pl.pallas_call(
        spread,
        out_shape=jax.ShapeDtypeStruct((2, nx, 2, width, half), slab_t.dtype),
        in_specs=[vmem],
        out_specs=anywhere,
        scratch_shapes=[pltpu.SemaphoreType.DMA((4 * nx,))],
    )(slab_t)
    mine = lax.all_to_all(copies.reshape(4 * nx, width, half), COL, 0, 0).reshape(4 * nx * width, half)
    h_all = lax.all_gather(jnp.concatenate([factor_h[0], factor_h[1]], axis=1), "z", axis=0, tiled=True)
    h_yl = lax.ppermute(h_all, "yl", SWAP)
    h_yh = lax.ppermute(h_all, "yh", SWAP)
    h_both = lax.ppermute(h_all, ("yl", "yh"), [(i, 3 - i) for i in range(4)])
    mine, h_yl, h_yh, h_both = lax.optimization_barrier((mine, h_yl, h_yh, h_both))

    index = jnp.stack([yh, c, x, yl]).astype(jnp.int32)
    params = pltpu.CompilerParams(vmem_limit_bytes=14 * 2**20)
    half_like = jax.ShapeDtypeStruct((width, rows), jnp.float32)
    cost = pl.CostEstimate(flops=2 * 16 * 2 * width * width * rows, bytes_accessed=8 * 2**20, transcendentals=0)

    gram_like = jax.ShapeDtypeStruct((nz, 2, 2, width // 4, 2 * width), jnp.float32)
    row_like = jax.ShapeDtypeStruct((nz, 2, width // 4, 2 * width), jnp.float32)
    core_terms = pl.pallas_call(
        other_core_gram,
        out_shape=gram_like,
        in_specs=[smem, vmem],
        out_specs=vmem,
        compiler_params=params,
        cost_estimate=cost,
    )(index, mine)
    core = lax.ppermute(mine, "c", SWAP)
    core_terms = lax.ppermute(core_terms, "c", SWAP)
    factor = pl.pallas_call(
        arrange,
        out_shape=jax.ShapeDtypeStruct((4 * nx * width, 2 * width), slab_t.dtype),
        in_specs=[smem] + [vmem] * 4,
        out_specs=vmem,
        compiler_params=params,
        cost_estimate=pl.CostEstimate(flops=0, bytes_accessed=2**20, transcendentals=0),
    )(index, h_all, h_yl, h_yh, h_both)
    terms, yl_terms = pl.pallas_call(
        this_core_gram,
        out_shape=(row_like, row_like),
        in_specs=[smem, vmem, vmem],
        out_specs=(vmem, vmem),
        compiler_params=params,
        cost_estimate=cost,
    )(index, mine, core_terms)
    yl_terms = lax.ppermute(yl_terms, "yl", SWAP)
    keep, send = pl.pallas_call(
        recon_products,
        out_shape=(half_like, half_like),
        in_specs=[smem] + [vmem] * 3,
        out_specs=(vmem,) * 2,
        compiler_params=params,
        cost_estimate=cost,
    )(index, mine, core, factor)
    terms, yl_terms, send = lax.optimization_barrier((terms, yl_terms, send))
    recon_other = lax.ppermute(send, "yh", SWAP)
    terms = terms + yl_terms
    local = width // 2
    parts = lax.all_to_all(terms.reshape(nrow, width // 4, 2 * width), ("z", "yh"), 0, 0)
    summed = parts.reshape(nz, 2, width // 4, 2, width).sum(0).transpose(2, 1, 0, 3).reshape(local, 2, width)

    slab = jnp.arange(2, dtype=jnp.int32)
    is_own = (slab == yh)[:, None, None]
    polar = target_t.astype(jnp.float32) - jnp.where(is_own, keep[None], recon_other[None])

    order_n = rows * nrow
    b_index = lax.axis_index(ROW) * local + jnp.arange(local, dtype=jnp.int32)
    a_index = lax.axis_index(COL) * width + jnp.arange(width, dtype=jnp.int32)
    identity = (b_index[:, None, None] == a_index[None, None, :]).astype(jnp.float32)
    gram = (summed - order_n * identity) * (1.0 / math.sqrt(order_n))
    return (gram, polar)


def solution(mesh):
    parts = Mesh(mesh.devices.reshape(16, 2, 2, 4, 2), AXES)
    return jax.shard_map(
        shards,
        mesh=parts,
        in_specs=(P(None, COL, ROW), P(None, COL, ROW), P(None, ROW, COL)),
        out_specs=(P(ROW, None, COL), P(None, COL, ROW)),
        check_vma=False,
    )
```

```python
import functools
import itertools
import math

import jax
import jax.numpy as jnp
from jax import lax
from jax.experimental import pallas as pl
from jax.experimental.pallas import tpu as pltpu
from jax.sharding import Mesh, PartitionSpec as P

AXES = ("z", "yl", "yh", "x", "c")
ROW = ("z", "yl")
COL = ("yh", "x", "c")
SWAP = [(0, 1), (1, 0)]


def spread(slab, copies, sems):
    half = copies.shape[4]
    started = []
    for yh, x, c in itertools.product(*map(range, copies.shape[:3])):
        source = slab.at[yh, :, pl.ds(c * half, half)]
        started.append(pltpu.make_async_copy(source, copies.at[yh, x, c], sems.at[len(started)]))
        started[-1].start()
    for copy in started:
        copy.wait()


def gram_products(index, mine, core):
    width = mine.shape[0] // 16
    c = index[1] if core == 0 else 1 - index[1]
    own = [mine[pl.ds(pl.multiple_of((8 * yh + 2 * index[2] + c) * width, width), width), :] for yh in range(2)]
    own = jnp.concatenate(own, axis=0)
    terms = lax.dot_general(mine[...], own, (((1,), (1,)), ((), ())), preferred_element_type=jnp.float32)
    terms = terms.reshape(-1, 2, 2, width // 4, 2 * width)
    parts = []
    for yh in range(2):
        columns = terms[..., yh * width:(yh + 1) * width]
        parts.append(jnp.concatenate([columns[:, :, 0], columns[:, :, 1]], axis=-1))
    return parts


def other_core_gram(index, mine, gram):
    for yh, part in enumerate(gram_products(index, mine, 1)):
        gram[:, :, yh] = part


def this_core_gram(index, mine, received, keep, send):
    for yh, part in enumerate(gram_products(index, mine, 0)):
        total = part + received[:, :, yh]
        keep[:, yh] = jnp.where(index[3] == 0, total[:, 0], total[:, 1])
        send[:, yh] = jnp.where(index[3] == 0, total[:, 1], total[:, 0])


def arrange(index, h, h_yl, h_yh, h_both, factor):
    width = factor.shape[1] // 2
    halves = []
    for parts in ((h, h_yh), (h_yl, h_both)):
        runs = [jnp.where(index[0] == 0, part[:, :width], part[:, width:]) for part in parts]
        halves.append(jnp.concatenate(runs, axis=1))
    pair = [jnp.where(index[3] == yl, halves[0], halves[1]).reshape(-1, width // 2, 2 * width) for yl in range(2)]
    factor[...] = jnp.stack(pair, axis=1).reshape(factor.shape)


def recon_here(rows, factor, recon):
    recon[...] = lax.dot_general(factor[...], rows[...], (((0,), (0,)), ((), ())), preferred_element_type=jnp.float32)


def recon_both(index, rows, factor, here, keep, send):
    width, half = keep.shape[0], rows.shape[1]
    there = lax.dot_general(factor[...], rows[...], (((0,), (0,)), ((), ())), preferred_element_type=jnp.float32)
    for at, out in enumerate((keep, send)):
        run = slice(at * width, (at + 1) * width)
        out[:, :half] = jnp.where(index[1] == 0, here[run, :], there[run])
        out[:, half:] = jnp.where(index[1] == 0, there[run], here[run, :])


def subtract(yh, target, recon, polar, scratch, sem):
    scratch[...] = target[yh].astype(jnp.float32) - recon[...]
    copy = pltpu.make_async_copy(scratch, polar.at[yh], sem)
    copy.start()
    copy.wait()


def finish_own(index, target, keep, polar, scratch, sem):
    subtract(index[0], target, keep, polar, scratch, sem)


def finish_other(index, target, recon, polar_in, polar, scratch, sem):
    subtract(1 - index[0], target, recon, polar, scratch, sem)


def shards(slab_t, target_t, factor_h):
    yh, x, c = (lax.axis_index(name) for name in COL)
    yl = lax.axis_index("yl")
    width, rows = slab_t.shape[1:]
    nrow, nz, nx = lax.axis_size(ROW), lax.axis_size("z"), lax.axis_size("x")
    half = rows // 2
    smem, vmem, anywhere = (pl.BlockSpec(memory_space=space) for space in (pltpu.SMEM, pltpu.VMEM, pl.ANY))
    copies = pl.pallas_call(
        spread,
        out_shape=jax.ShapeDtypeStruct((2, nx, 2, width, half), slab_t.dtype),
        in_specs=[vmem],
        out_specs=anywhere,
        scratch_shapes=[pltpu.SemaphoreType.DMA((4 * nx,))],
    )(slab_t)
    mine = lax.all_to_all(copies.reshape(4 * nx, width, half), COL, 0, 0).reshape(4 * nx * width, half)
    h_all = lax.all_gather(jnp.concatenate([factor_h[0], factor_h[1]], axis=1), "z", axis=0, tiled=True)
    h_yl = lax.ppermute(h_all, "yl", SWAP)
    h_yh = lax.ppermute(h_all, "yh", SWAP)
    h_both = lax.ppermute(h_all, ("yl", "yh"), [(i, 3 - i) for i in range(4)])
    mine, h_yl, h_yh, h_both = lax.optimization_barrier((mine, h_yl, h_yh, h_both))

    index = jnp.stack([yh, c, x, yl]).astype(jnp.int32)
    params = pltpu.CompilerParams(vmem_limit_bytes=14 * 2**20)
    half_like = jax.ShapeDtypeStruct((width, rows), jnp.float32)
    cost = pl.CostEstimate(flops=2 * 16 * 2 * width * width * rows, bytes_accessed=8 * 2**20, transcendentals=0)

    gram_like = jax.ShapeDtypeStruct((nz, 2, 2, width // 4, 2 * width), jnp.float32)
    row_like = jax.ShapeDtypeStruct((nz, 2, width // 4, 2 * width), jnp.float32)
    core_terms = pl.pallas_call(
        other_core_gram,
        out_shape=gram_like,
        in_specs=[smem, vmem],
        out_specs=vmem,
        compiler_params=params,
        cost_estimate=cost,
    )(index, mine)
    core_terms = lax.ppermute(core_terms, "c", SWAP)
    terms, yl_terms = pl.pallas_call(
        this_core_gram,
        out_shape=(row_like, row_like),
        in_specs=[smem, vmem, vmem],
        out_specs=(vmem, vmem),
        compiler_params=params,
        cost_estimate=cost,
    )(index, mine, core_terms)
    terms, yl_terms, mine, h_all = lax.optimization_barrier((terms, yl_terms, mine, h_all))
    yl_terms = lax.ppermute(yl_terms, "yl", SWAP)
    core = lax.ppermute(mine, "c", SWAP)
    factor = pl.pallas_call(
        arrange,
        out_shape=jax.ShapeDtypeStruct((4 * nx * width, 2 * width), slab_t.dtype),
        in_specs=[smem] + [vmem] * 4,
        out_specs=vmem,
        compiler_params=params,
        cost_estimate=pl.CostEstimate(flops=0, bytes_accessed=2**20, transcendentals=0),
    )(index, h_all, h_yl, h_yh, h_both)
    here = pl.pallas_call(
        recon_here,
        out_shape=jax.ShapeDtypeStruct((2 * width, half), jnp.float32),
        in_specs=[vmem] * 2,
        out_specs=vmem,
        compiler_params=params,
        cost_estimate=cost,
    )(mine, factor)
    keep, send = pl.pallas_call(
        recon_both,
        out_shape=(half_like, half_like),
        in_specs=[smem] + [vmem] * 3,
        out_specs=(vmem,) * 2,
        compiler_params=params,
        cost_estimate=cost,
    )(index, core, factor, here)
    recon_other = lax.ppermute(send, "yh", SWAP)
    terms, yl_terms, send = lax.optimization_barrier((terms, yl_terms, send))
    terms = terms + yl_terms
    local = width // 2
    parts = lax.all_to_all(terms.reshape(nrow, width // 4, 2 * width), ("z", "yh"), 0, 0)
    summed = parts.reshape(nz, 2, width // 4, 2, width).sum(0).transpose(2, 1, 0, 3).reshape(local, 2, width)

    def finish(kernel, *args, **kwargs):
        return pl.pallas_call(
            kernel,
            out_shape=jax.ShapeDtypeStruct(target_t.shape, jnp.float32),
            in_specs=[smem, vmem, vmem] + [anywhere] * (len(args) - 1),
            out_specs=anywhere,
            scratch_shapes=[pltpu.VMEM((width, rows), jnp.float32), pltpu.SemaphoreType.DMA],
            compiler_params=params,
            cost_estimate=pl.CostEstimate(flops=width * rows, bytes_accessed=10 * width * rows, transcendentals=0),
            **kwargs,
        )(index, target_t, *args)

    polar = finish(finish_own, keep)

    order_n = rows * nrow
    b_index = lax.axis_index(ROW) * local + jnp.arange(local, dtype=jnp.int32)
    a_index = lax.axis_index(COL) * width + jnp.arange(width, dtype=jnp.int32)
    identity = (b_index[:, None, None] == a_index[None, None, :]).astype(jnp.float32)
    gram = (summed - order_n * identity) * (1.0 / math.sqrt(order_n))
    gram, recon_other, polar = lax.optimization_barrier((gram, recon_other, polar))
    polar = finish(finish_other, recon_other, polar, input_output_aliases={3: 0})
    return (gram, polar)


def solution(mesh):
    parts = Mesh(mesh.devices.reshape(16, 2, 2, 4, 2), AXES)
    return jax.shard_map(
        shards,
        mesh=parts,
        in_specs=(P(None, COL, ROW), P(None, COL, ROW), P(None, ROW, COL)),
        out_specs=(P(ROW, None, COL), P(None, COL, ROW)),
        check_vma=False,
    )
```

```python
import functools
import itertools
import math

import jax
import jax.numpy as jnp
from jax import lax
from jax.experimental import pallas as pl
from jax.experimental.pallas import tpu as pltpu
from jax.sharding import Mesh, PartitionSpec as P

AXES = ("z", "yl", "yh", "x", "c")
ROW = ("z", "yl")
COL = ("yh", "x", "c")
SWAP = [(0, 1), (1, 0)]


def spread(slab, copies, sems):
    half = copies.shape[4]
    started = []
    for yh, x, c in itertools.product(*map(range, copies.shape[:3])):
        source = slab.at[yh, :, pl.ds(c * half, half)]
        started.append(pltpu.make_async_copy(source, copies.at[yh, x, c], sems.at[len(started)]))
        started[-1].start()
    for copy in started:
        copy.wait()


def gram_products(index, mine, core):
    width = mine.shape[0] // 16
    c = index[1] if core == 0 else 1 - index[1]
    own = [mine[pl.ds(pl.multiple_of((8 * yh + 2 * index[2] + c) * width, width), width), :] for yh in range(2)]
    own = jnp.concatenate(own, axis=0)
    terms = lax.dot_general(mine[...], own, (((1,), (1,)), ((), ())), preferred_element_type=jnp.float32)
    terms = terms.reshape(-1, 2, 2, width // 4, 2 * width)
    parts = []
    for yh in range(2):
        columns = terms[..., yh * width:(yh + 1) * width]
        parts.append(jnp.concatenate([columns[:, :, 0], columns[:, :, 1]], axis=-1))
    return parts


def other_core_gram(index, mine, gram):
    for yh, part in enumerate(gram_products(index, mine, 1)):
        gram[:, :, yh] = part


def this_core_gram(index, mine, received, keep, send):
    for yh, part in enumerate(gram_products(index, mine, 0)):
        total = part + received[:, :, yh]
        keep[:, yh] = jnp.where(index[3] == 0, total[:, 0], total[:, 1])
        send[:, yh] = jnp.where(index[3] == 0, total[:, 1], total[:, 0])


def arrange(index, h, h_yl, h_yh, h_both, factor):
    width = factor.shape[1] // 2
    halves = []
    for parts in ((h, h_yh), (h_yl, h_both)):
        runs = [jnp.where(index[0] == 0, part[:, :width], part[:, width:]) for part in parts]
        halves.append(jnp.concatenate(runs, axis=1))
    pair = [jnp.where(index[3] == yl, halves[0], halves[1]).reshape(-1, width // 2, 2 * width) for yl in range(2)]
    factor[...] = jnp.stack(pair, axis=1).reshape(factor.shape)


def recon_here(rows, factor, recon):
    recon[...] = lax.dot_general(factor[...], rows[...], (((0,), (0,)), ((), ())), preferred_element_type=jnp.float32)


def recon_both(index, rows, factor, here, keep, send):
    width, half = keep.shape[0], rows.shape[1]
    there = lax.dot_general(factor[...], rows[...], (((0,), (0,)), ((), ())), preferred_element_type=jnp.float32)
    for at, out in enumerate((keep, send)):
        run = slice(at * width, (at + 1) * width)
        out[:, :half] = jnp.where(index[1] == 0, here[run, :], there[run])
        out[:, half:] = jnp.where(index[1] == 0, there[run], here[run, :])


def subtract(yh, target, recon, polar, scratch, sem):
    scratch[...] = target[yh].astype(jnp.float32) - recon[...]
    copy = pltpu.make_async_copy(scratch, polar.at[yh], sem)
    copy.start()
    copy.wait()


def finish_own(index, target, keep, polar, scratch, sem):
    subtract(index[0], target, keep, polar, scratch, sem)


def finish_other(index, target, recon, polar_in, polar, scratch, sem):
    subtract(1 - index[0], target, recon, polar, scratch, sem)


def shards(slab_t, target_t, factor_h):
    yh, x, c = (lax.axis_index(name) for name in COL)
    yl = lax.axis_index("yl")
    width, rows = slab_t.shape[1:]
    nrow, nz, nx = lax.axis_size(ROW), lax.axis_size("z"), lax.axis_size("x")
    half = rows // 2
    smem, vmem, anywhere = (pl.BlockSpec(memory_space=space) for space in (pltpu.SMEM, pltpu.VMEM, pl.ANY))
    copies = pl.pallas_call(
        spread,
        out_shape=jax.ShapeDtypeStruct((2, nx, 2, width, half), slab_t.dtype),
        in_specs=[vmem],
        out_specs=anywhere,
        scratch_shapes=[pltpu.SemaphoreType.DMA((4 * nx,))],
    )(slab_t)
    mine = lax.all_to_all(copies.reshape(4 * nx, width, half), COL, 0, 0).reshape(4 * nx * width, half)
    h_all = lax.all_gather(jnp.concatenate([factor_h[0], factor_h[1]], axis=1), "z", axis=0, tiled=True)
    h_both = lax.ppermute(h_all, ("yl", "yh"), [(i, 3 - i) for i in range(4)])
    h_yh = lax.ppermute(h_all, "yh", SWAP)
    h_yl = lax.ppermute(h_all, "yl", SWAP)
    mine, h_both, h_yh, h_yl = lax.optimization_barrier((mine, h_both, h_yh, h_yl))

    index = jnp.stack([yh, c, x, yl]).astype(jnp.int32)
    params = pltpu.CompilerParams(vmem_limit_bytes=14 * 2**20)
    half_like = jax.ShapeDtypeStruct((width, rows), jnp.float32)
    cost = pl.CostEstimate(flops=2 * 16 * 2 * width * width * rows, bytes_accessed=8 * 2**20, transcendentals=0)

    gram_like = jax.ShapeDtypeStruct((nz, 2, 2, width // 4, 2 * width), jnp.float32)
    row_like = jax.ShapeDtypeStruct((nz, 2, width // 4, 2 * width), jnp.float32)
    core_terms = pl.pallas_call(
        other_core_gram,
        out_shape=gram_like,
        in_specs=[smem, vmem],
        out_specs=vmem,
        compiler_params=params,
        cost_estimate=cost,
    )(index, mine)
    core_terms = lax.ppermute(core_terms, "c", SWAP)
    terms, yl_terms = pl.pallas_call(
        this_core_gram,
        out_shape=(row_like, row_like),
        in_specs=[smem, vmem, vmem],
        out_specs=(vmem, vmem),
        compiler_params=params,
        cost_estimate=cost,
    )(index, mine, core_terms)
    terms, yl_terms, mine, h_all = lax.optimization_barrier((terms, yl_terms, mine, h_all))
    yl_terms = lax.ppermute(yl_terms, "yl", SWAP)
    core = lax.ppermute(mine, "c", SWAP)
    factor = pl.pallas_call(
        arrange,
        out_shape=jax.ShapeDtypeStruct((4 * nx * width, 2 * width), slab_t.dtype),
        in_specs=[smem] + [vmem] * 4,
        out_specs=vmem,
        compiler_params=params,
        cost_estimate=pl.CostEstimate(flops=0, bytes_accessed=2**20, transcendentals=0),
    )(index, h_all, h_yl, h_yh, h_both)
    here = pl.pallas_call(
        recon_here,
        out_shape=jax.ShapeDtypeStruct((2 * width, half), jnp.float32),
        in_specs=[vmem] * 2,
        out_specs=vmem,
        compiler_params=params,
        cost_estimate=cost,
    )(mine, factor)
    keep, send = pl.pallas_call(
        recon_both,
        out_shape=(half_like, half_like),
        in_specs=[smem] + [vmem] * 3,
        out_specs=(vmem,) * 2,
        compiler_params=params,
        cost_estimate=cost,
    )(index, core, factor, here)
    recon_other = lax.ppermute(send, "yh", SWAP)
    terms, yl_terms, send = lax.optimization_barrier((terms, yl_terms, send))
    terms = terms + yl_terms
    local = width // 2
    parts = lax.all_to_all(terms, "z", 0, 0)

    def finish(kernel, *args, **kwargs):
        return pl.pallas_call(
            kernel,
            out_shape=jax.ShapeDtypeStruct(target_t.shape, jnp.float32),
            in_specs=[smem, vmem, vmem] + [anywhere] * (len(args) - 1),
            out_specs=anywhere,
            scratch_shapes=[pltpu.VMEM((width, rows), jnp.float32), pltpu.SemaphoreType.DMA],
            compiler_params=params,
            cost_estimate=pl.CostEstimate(flops=width * rows, bytes_accessed=10 * width * rows, transcendentals=0),
            **kwargs,
        )(index, target_t, *args)

    polar = finish(finish_own, keep)
    parts, polar = lax.optimization_barrier((parts, polar))
    parts = parts.sum(0)
    own_part = lax.dynamic_index_in_dim(parts, yh, 0, keepdims=False)
    other_part = lax.ppermute(lax.dynamic_index_in_dim(parts, 1 - yh, 0, keepdims=False), "yh", SWAP)
    own_part, recon_other, polar = lax.optimization_barrier((own_part, recon_other, polar))
    polar = finish(finish_other, recon_other, polar, input_output_aliases={3: 0})
    is_own = (jnp.arange(2, dtype=jnp.int32) == yh)[:, None, None]
    parts = jnp.where(is_own, own_part[None], other_part[None])
    summed = parts.reshape(2, width // 4, 2, width).transpose(2, 1, 0, 3).reshape(local, 2, width)

    order_n = rows * nrow
    b_index = lax.axis_index(ROW) * local + jnp.arange(local, dtype=jnp.int32)
    a_index = lax.axis_index(COL) * width + jnp.arange(width, dtype=jnp.int32)
    identity = (b_index[:, None, None] == a_index[None, None, :]).astype(jnp.float32)
    gram = (summed - order_n * identity) * (1.0 / math.sqrt(order_n))
    return (gram, polar)


def solution(mesh):
    parts = Mesh(mesh.devices.reshape(16, 2, 2, 4, 2), AXES)
    return jax.shard_map(
        shards,
        mesh=parts,
        in_specs=(P(None, COL, ROW), P(None, COL, ROW), P(None, ROW, COL)),
        out_specs=(P(ROW, None, COL), P(None, COL, ROW)),
        check_vma=False,
    )
```

```python
import functools
import itertools
import math

import jax
import jax.numpy as jnp
from jax import lax
from jax.experimental import pallas as pl
from jax.experimental.pallas import tpu as pltpu
from jax.sharding import Mesh, PartitionSpec as P

AXES = ("z", "yl", "yh", "x", "c")
ROW = ("z", "yl")
COL = ("yh", "x", "c")
SWAP = [(0, 1), (1, 0)]


def spread(slab, copies, pieces, load_sems, sems):
    half = copies.shape[4]
    loads, started = [], []
    for yh, c in itertools.product(range(2), range(2)):
        source = slab.at[yh, :, pl.ds(c * half, half)]
        loads.append((yh, c, pltpu.make_async_copy(source, pieces.at[yh, c], load_sems.at[len(loads)])))
        loads[-1][2].start()
    for yh, c, load in loads:
        load.wait()
        for x in range(copies.shape[1]):
            started.append(pltpu.make_async_copy(pieces.at[yh, c], copies.at[yh, x, c], sems.at[len(started)]))
            started[-1].start()
    for copy in started:
        copy.wait()


def gram_products(index, mine, core):
    width = mine.shape[0] // 16
    c = index[1] if core == 0 else 1 - index[1]
    own = [mine[pl.ds(pl.multiple_of((8 * yh + 2 * index[2] + c) * width, width), width), :] for yh in range(2)]
    own = jnp.concatenate(own, axis=0)
    terms = lax.dot_general(mine[...], own, (((1,), (1,)), ((), ())), preferred_element_type=jnp.float32)
    terms = terms.reshape(-1, 2, 2, width // 4, 2 * width)
    parts = []
    for yh in range(2):
        columns = terms[..., yh * width:(yh + 1) * width]
        parts.append(jnp.concatenate([columns[:, :, 0], columns[:, :, 1]], axis=-1))
    return parts


def other_core_gram(index, mine, gram):
    for yh, part in enumerate(gram_products(index, mine, 1)):
        gram[:, :, yh] = part


def this_core_gram(index, mine, received, keep, send):
    for yh, part in enumerate(gram_products(index, mine, 0)):
        total = part + received[:, :, yh]
        keep[:, yh] = jnp.where(index[3] == 0, total[:, 0], total[:, 1])
        send[:, yh] = jnp.where(index[3] == 0, total[:, 1], total[:, 0])


def arrange(index, h, h_yl, h_yh, h_both, factor):
    width = factor.shape[1] // 2
    halves = []
    for parts in ((h, h_yh), (h_yl, h_both)):
        runs = [jnp.where(index[0] == 0, part[:, :width], part[:, width:]) for part in parts]
        halves.append(jnp.concatenate(runs, axis=1))
    pair = [jnp.where(index[3] == yl, halves[0], halves[1]).reshape(-1, width // 2, 2 * width) for yl in range(2)]
    factor[...] = jnp.stack(pair, axis=1).reshape(factor.shape)


def recon_here(rows, factor, recon):
    recon[...] = lax.dot_general(factor[...], rows[...], (((0,), (0,)), ((), ())), preferred_element_type=jnp.float32)


def recon_both(index, rows, factor, here, keep, send):
    width, half = keep.shape[0], rows.shape[1]
    there = lax.dot_general(factor[...], rows[...], (((0,), (0,)), ((), ())), preferred_element_type=jnp.float32)
    for at, out in enumerate((keep, send)):
        run = slice(at * width, (at + 1) * width)
        out[:, :half] = jnp.where(index[1] == 0, here[run, :], there[run])
        out[:, half:] = jnp.where(index[1] == 0, there[run], here[run, :])


def subtract(yh, target, recon, polar, scratch, sem):
    scratch[...] = target[yh].astype(jnp.float32) - recon[...]
    copy = pltpu.make_async_copy(scratch, polar.at[yh], sem)
    copy.start()
    copy.wait()


def finish_own(index, target, keep, polar, scratch, sem):
    subtract(index[0], target, keep, polar, scratch, sem)


def finish_other(index, target, recon, polar_in, polar, scratch, sem):
    subtract(1 - index[0], target, recon, polar, scratch, sem)


def shards(slab_t, target_t, factor_h):
    yh, x, c = (lax.axis_index(name) for name in COL)
    yl = lax.axis_index("yl")
    width, rows = slab_t.shape[1:]
    nrow, nz, nx = lax.axis_size(ROW), lax.axis_size("z"), lax.axis_size("x")
    half = rows // 2
    smem, vmem, anywhere = (pl.BlockSpec(memory_space=space) for space in (pltpu.SMEM, pltpu.VMEM, pl.ANY))
    copies = pl.pallas_call(
        spread,
        out_shape=jax.ShapeDtypeStruct((2, nx, 2, width, half), slab_t.dtype),
        in_specs=[anywhere],
        out_specs=anywhere,
        scratch_shapes=[
            pltpu.VMEM((2, 2, width, half), slab_t.dtype),
            pltpu.SemaphoreType.DMA((4,)),
            pltpu.SemaphoreType.DMA((4 * nx,)),
        ],
    )(slab_t)
    mine = lax.all_to_all(copies.reshape(4 * nx, width, half), COL, 0, 0).reshape(4 * nx * width, half)
    h_all = lax.all_gather(jnp.concatenate([factor_h[0], factor_h[1]], axis=1), "z", axis=0, tiled=True)
    h_both = lax.ppermute(h_all, ("yl", "yh"), [(i, 3 - i) for i in range(4)])
    h_yh = lax.ppermute(h_all, "yh", SWAP)
    h_yl = lax.ppermute(h_all, "yl", SWAP)
    mine, h_both, h_yh, h_yl = lax.optimization_barrier((mine, h_both, h_yh, h_yl))

    index = jnp.stack([yh, c, x, yl]).astype(jnp.int32)
    params = pltpu.CompilerParams(vmem_limit_bytes=14 * 2**20)
    half_like = jax.ShapeDtypeStruct((width, rows), jnp.float32)
    cost = pl.CostEstimate(flops=2 * 16 * 2 * width * width * rows, bytes_accessed=8 * 2**20, transcendentals=0)

    gram_like = jax.ShapeDtypeStruct((nz, 2, 2, width // 4, 2 * width), jnp.float32)
    row_like = jax.ShapeDtypeStruct((nz, 2, width // 4, 2 * width), jnp.float32)
    core_terms = pl.pallas_call(
        other_core_gram,
        out_shape=gram_like,
        in_specs=[smem, vmem],
        out_specs=vmem,
        compiler_params=params,
        cost_estimate=cost,
    )(index, mine)
    core_terms = lax.ppermute(core_terms, "c", SWAP)
    terms, yl_terms = pl.pallas_call(
        this_core_gram,
        out_shape=(row_like, row_like),
        in_specs=[smem, vmem, vmem],
        out_specs=(vmem, vmem),
        compiler_params=params,
        cost_estimate=cost,
    )(index, mine, core_terms)
    terms, yl_terms, mine, h_all = lax.optimization_barrier((terms, yl_terms, mine, h_all))
    yl_terms = lax.ppermute(yl_terms, "yl", SWAP)
    core = lax.ppermute(mine, "c", SWAP)
    factor = pl.pallas_call(
        arrange,
        out_shape=jax.ShapeDtypeStruct((4 * nx * width, 2 * width), slab_t.dtype),
        in_specs=[smem] + [vmem] * 4,
        out_specs=vmem,
        compiler_params=params,
        cost_estimate=pl.CostEstimate(flops=0, bytes_accessed=2**20, transcendentals=0),
    )(index, h_all, h_yl, h_yh, h_both)
    here = pl.pallas_call(
        recon_here,
        out_shape=jax.ShapeDtypeStruct((2 * width, half), jnp.float32),
        in_specs=[vmem] * 2,
        out_specs=vmem,
        compiler_params=params,
        cost_estimate=cost,
    )(mine, factor)
    keep, send = pl.pallas_call(
        recon_both,
        out_shape=(half_like, half_like),
        in_specs=[smem] + [vmem] * 3,
        out_specs=(vmem,) * 2,
        compiler_params=params,
        cost_estimate=cost,
    )(index, core, factor, here)
    recon_other = lax.ppermute(send, "yh", SWAP)
    terms, yl_terms, send = lax.optimization_barrier((terms, yl_terms, send))
    terms = terms + yl_terms
    local = width // 2
    parts = lax.all_to_all(terms, "z", 0, 0)

    def finish(kernel, *args, **kwargs):
        return pl.pallas_call(
            kernel,
            out_shape=jax.ShapeDtypeStruct(target_t.shape, jnp.float32),
            in_specs=[smem, vmem, vmem] + [anywhere] * (len(args) - 1),
            out_specs=anywhere,
            scratch_shapes=[pltpu.VMEM((width, rows), jnp.float32), pltpu.SemaphoreType.DMA],
            compiler_params=params,
            cost_estimate=pl.CostEstimate(flops=width * rows, bytes_accessed=10 * width * rows, transcendentals=0),
            **kwargs,
        )(index, target_t, *args)

    polar = finish(finish_own, keep)
    parts, polar = lax.optimization_barrier((parts, polar))
    parts = parts.sum(0)
    own_part = lax.dynamic_index_in_dim(parts, yh, 0, keepdims=False)
    other_part = lax.ppermute(lax.dynamic_index_in_dim(parts, 1 - yh, 0, keepdims=False), "yh", SWAP)
    own_part, recon_other, polar = lax.optimization_barrier((own_part, recon_other, polar))
    polar = finish(finish_other, recon_other, polar, input_output_aliases={3: 0})
    is_own = (jnp.arange(2, dtype=jnp.int32) == yh)[:, None, None]
    parts = jnp.where(is_own, own_part[None], other_part[None])
    summed = parts.reshape(2, width // 4, 2, width).transpose(2, 1, 0, 3).reshape(local, 2, width)

    order_n = rows * nrow
    b_index = lax.axis_index(ROW) * local + jnp.arange(local, dtype=jnp.int32)
    a_index = lax.axis_index(COL) * width + jnp.arange(width, dtype=jnp.int32)
    identity = (b_index[:, None, None] == a_index[None, None, :]).astype(jnp.float32)
    gram = (summed - order_n * identity) * (1.0 / math.sqrt(order_n))
    return (gram, polar)


def solution(mesh):
    parts = Mesh(mesh.devices.reshape(16, 2, 2, 4, 2), AXES)
    return jax.shard_map(
        shards,
        mesh=parts,
        in_specs=(P(None, COL, ROW), P(None, COL, ROW), P(None, ROW, COL)),
        out_specs=(P(ROW, None, COL), P(None, COL, ROW)),
        check_vma=False,
    )
```

```python
import functools
import itertools
import math

import jax
import jax.numpy as jnp
from jax import lax
from jax.experimental import pallas as pl
from jax.experimental.pallas import tpu as pltpu
from jax.sharding import Mesh, PartitionSpec as P

AXES = ("z", "yl", "yh", "x", "c")
ROW = ("z", "yl")
COL = ("yh", "x", "c")
SWAP = [(0, 1), (1, 0)]


def spread(slab, copies, pieces, load_sems, sems):
    half = copies.shape[4]
    loads, started = [], []
    for yh, c in itertools.product(range(2), range(2)):
        source = slab.at[yh, :, pl.ds(c * half, half)]
        loads.append((yh, c, pltpu.make_async_copy(source, pieces.at[yh, c], load_sems.at[len(loads)])))
        loads[-1][2].start()
    for yh, c, load in loads:
        load.wait()
        for x in range(copies.shape[1]):
            started.append(pltpu.make_async_copy(pieces.at[yh, c], copies.at[yh, x, c], sems.at[len(started)]))
            started[-1].start()
    for copy in started:
        copy.wait()


def gram_products(index, mine, core):
    width = mine.shape[0] // 16
    c = index[1] if core == 0 else 1 - index[1]
    own = [mine[pl.ds(pl.multiple_of((8 * yh + 2 * index[2] + c) * width, width), width), :] for yh in range(2)]
    own = jnp.concatenate(own, axis=0)
    terms = lax.dot_general(mine[...], own, (((1,), (1,)), ((), ())), preferred_element_type=jnp.float32)
    terms = terms.reshape(-1, 2, 2, width // 4, 2 * width)
    parts = []
    for yh in range(2):
        columns = terms[..., yh * width:(yh + 1) * width]
        parts.append(jnp.concatenate([columns[:, :, 0], columns[:, :, 1]], axis=-1))
    return parts


def other_core_gram(index, mine, gram):
    for yh, part in enumerate(gram_products(index, mine, 1)):
        gram[:, :, yh] = part


def this_core_gram(index, mine, received, keep, send):
    for yh, part in enumerate(gram_products(index, mine, 0)):
        total = part + received[:, :, yh]
        keep[:, yh] = jnp.where(index[3] == 0, total[:, 0], total[:, 1])
        send[:, yh] = jnp.where(index[3] == 0, total[:, 1], total[:, 0])


def arrange(index, h, h_yl, h_yh, h_both, factor):
    width = factor.shape[1] // 2
    halves = []
    for parts in ((h, h_yh), (h_yl, h_both)):
        runs = [jnp.where(index[0] == 0, part[:, :width], part[:, width:]) for part in parts]
        halves.append(jnp.concatenate(runs, axis=1))
    pair = [jnp.where(index[3] == yl, halves[0], halves[1]).reshape(-1, width // 2, 2 * width) for yl in range(2)]
    factor[...] = jnp.stack(pair, axis=1).reshape(factor.shape)


def recon_here(rows, factor, recon):
    recon[...] = lax.dot_general(factor[...], rows[...], (((0,), (0,)), ((), ())), preferred_element_type=jnp.float32)


def recon_both(index, rows, factor, here, keep, send):
    width, half = keep.shape[0], rows.shape[1]
    there = lax.dot_general(factor[...], rows[...], (((0,), (0,)), ((), ())), preferred_element_type=jnp.float32)
    for at, out in enumerate((keep, send)):
        run = slice(at * width, (at + 1) * width)
        out[:, :half] = jnp.where(index[1] == 0, here[run, :], there[run])
        out[:, half:] = jnp.where(index[1] == 0, there[run], here[run, :])


def subtract(yh, target, recon, polar, scratch, sem):
    size = scratch.shape[0] // 4
    copies = []
    for part in range(4):
        run = pl.ds(part * size, size)
        scratch[run, :] = target[yh, run, :].astype(jnp.float32) - recon[run, :]
        copies.append(pltpu.make_async_copy(scratch.at[run, :], polar.at[yh, run, :], sem.at[part]))
        copies[-1].start()
    for copy in copies:
        copy.wait()


def finish_own(index, target, keep, polar, scratch, sem):
    subtract(index[0], target, keep, polar, scratch, sem)


def finish_other(index, target, recon, polar_in, polar, scratch, sem):
    subtract(1 - index[0], target, recon, polar, scratch, sem)


def shards(slab_t, target_t, factor_h):
    yh, x, c = (lax.axis_index(name) for name in COL)
    yl = lax.axis_index("yl")
    width, rows = slab_t.shape[1:]
    nrow, nz, nx = lax.axis_size(ROW), lax.axis_size("z"), lax.axis_size("x")
    half = rows // 2
    smem, vmem, anywhere = (pl.BlockSpec(memory_space=space) for space in (pltpu.SMEM, pltpu.VMEM, pl.ANY))
    copies = pl.pallas_call(
        spread,
        out_shape=jax.ShapeDtypeStruct((2, nx, 2, width, half), slab_t.dtype),
        in_specs=[anywhere],
        out_specs=anywhere,
        scratch_shapes=[
            pltpu.VMEM((2, 2, width, half), slab_t.dtype),
            pltpu.SemaphoreType.DMA((4,)),
            pltpu.SemaphoreType.DMA((4 * nx,)),
        ],
    )(slab_t)
    mine = lax.all_to_all(copies.reshape(4 * nx, width, half), COL, 0, 0).reshape(4 * nx * width, half)
    h_all = lax.all_gather(jnp.concatenate([factor_h[0], factor_h[1]], axis=1), "z", axis=0, tiled=True)
    h_both = lax.ppermute(h_all, ("yl", "yh"), [(i, 3 - i) for i in range(4)])
    h_yh = lax.ppermute(h_all, "yh", SWAP)
    h_yl = lax.ppermute(h_all, "yl", SWAP)
    mine, h_both, h_yh, h_yl = lax.optimization_barrier((mine, h_both, h_yh, h_yl))

    index = jnp.stack([yh, c, x, yl]).astype(jnp.int32)
    params = pltpu.CompilerParams(vmem_limit_bytes=14 * 2**20)
    half_like = jax.ShapeDtypeStruct((width, rows), jnp.float32)
    cost = pl.CostEstimate(flops=2 * 16 * 2 * width * width * rows, bytes_accessed=8 * 2**20, transcendentals=0)

    gram_like = jax.ShapeDtypeStruct((nz, 2, 2, width // 4, 2 * width), jnp.float32)
    row_like = jax.ShapeDtypeStruct((nz, 2, width // 4, 2 * width), jnp.float32)
    core_terms = pl.pallas_call(
        other_core_gram,
        out_shape=gram_like,
        in_specs=[smem, vmem],
        out_specs=vmem,
        compiler_params=params,
        cost_estimate=cost,
    )(index, mine)
    core_terms = lax.ppermute(core_terms, "c", SWAP)
    terms, yl_terms = pl.pallas_call(
        this_core_gram,
        out_shape=(row_like, row_like),
        in_specs=[smem, vmem, vmem],
        out_specs=(vmem, vmem),
        compiler_params=params,
        cost_estimate=cost,
    )(index, mine, core_terms)
    terms, yl_terms, mine, h_all = lax.optimization_barrier((terms, yl_terms, mine, h_all))
    yl_terms = lax.ppermute(yl_terms, "yl", SWAP)
    core = lax.ppermute(mine, "c", SWAP)
    factor = pl.pallas_call(
        arrange,
        out_shape=jax.ShapeDtypeStruct((4 * nx * width, 2 * width), slab_t.dtype),
        in_specs=[smem] + [vmem] * 4,
        out_specs=vmem,
        compiler_params=params,
        cost_estimate=pl.CostEstimate(flops=0, bytes_accessed=2**20, transcendentals=0),
    )(index, h_all, h_yl, h_yh, h_both)
    here = pl.pallas_call(
        recon_here,
        out_shape=jax.ShapeDtypeStruct((2 * width, half), jnp.float32),
        in_specs=[vmem] * 2,
        out_specs=vmem,
        compiler_params=params,
        cost_estimate=cost,
    )(mine, factor)
    keep, send = pl.pallas_call(
        recon_both,
        out_shape=(half_like, half_like),
        in_specs=[smem] + [vmem] * 3,
        out_specs=(vmem,) * 2,
        compiler_params=params,
        cost_estimate=cost,
    )(index, core, factor, here)
    recon_other = lax.ppermute(send, "yh", SWAP)
    terms, yl_terms, send = lax.optimization_barrier((terms, yl_terms, send))
    terms = terms + yl_terms
    local = width // 2
    parts = lax.all_to_all(terms, "z", 0, 0)

    def finish(kernel, *args, **kwargs):
        return pl.pallas_call(
            kernel,
            out_shape=jax.ShapeDtypeStruct(target_t.shape, jnp.float32),
            in_specs=[smem, vmem, vmem] + [anywhere] * (len(args) - 1),
            out_specs=anywhere,
            scratch_shapes=[pltpu.VMEM((width, rows), jnp.float32), pltpu.SemaphoreType.DMA((4,))],
            compiler_params=params,
            cost_estimate=pl.CostEstimate(flops=width * rows, bytes_accessed=10 * width * rows, transcendentals=0),
            **kwargs,
        )(index, target_t, *args)

    polar = finish(finish_own, keep)
    parts, polar = lax.optimization_barrier((parts, polar))
    parts = parts.sum(0)
    own_part = lax.dynamic_index_in_dim(parts, yh, 0, keepdims=False)
    other_part = lax.ppermute(lax.dynamic_index_in_dim(parts, 1 - yh, 0, keepdims=False), "yh", SWAP)
    own_part, recon_other, polar = lax.optimization_barrier((own_part, recon_other, polar))
    polar = finish(finish_other, recon_other, polar, input_output_aliases={3: 0})
    is_own = (jnp.arange(2, dtype=jnp.int32) == yh)[:, None, None]
    parts = jnp.where(is_own, own_part[None], other_part[None])
    summed = parts.reshape(2, width // 4, 2, width).transpose(2, 1, 0, 3).reshape(local, 2, width)

    order_n = rows * nrow
    b_index = lax.axis_index(ROW) * local + jnp.arange(local, dtype=jnp.int32)
    a_index = lax.axis_index(COL) * width + jnp.arange(width, dtype=jnp.int32)
    identity = (b_index[:, None, None] == a_index[None, None, :]).astype(jnp.float32)
    gram = (summed - order_n * identity) * (1.0 / math.sqrt(order_n))
    return (gram, polar)


def solution(mesh):
    parts = Mesh(mesh.devices.reshape(16, 2, 2, 4, 2), AXES)
    return jax.shard_map(
        shards,
        mesh=parts,
        in_specs=(P(None, COL, ROW), P(None, COL, ROW), P(None, ROW, COL)),
        out_specs=(P(ROW, None, COL), P(None, COL, ROW)),
        check_vma=False,
    )
```
